32 devices in a mesh: group: 2 (over x), node: 16 (over z, y, core).
Axes of the slice: x: 2, y: 2, z: 4, core: 2. Of those that a mesh axis runs over, the one named last changes fastest.
Arguments:
- tokens: bfloat16 [512, 7168], P(('group', 'node')), parts along dimension 0, may hold values from -6 to 6
- expert_ids: int32 [512, 4], P(('group', 'node')), parts along dimension 0, may hold values from 0 to 7, as said below
- gates: bfloat16 [512, 4], P(('group', 'node')), parts along dimension 0, may hold values from 0.099609375 to 1
- expert_place: int32 [8], replicated, may hold values from 0 to 7, each once
- gate_proj: bfloat16 [7168, 8192], P(None, 'node'), may hold values from -0.0625 to 0.0625
- up_proj: bfloat16 [7168, 8192], P(None, 'node'), may hold values from -0.0625 to 0.0625
- down_proj: bfloat16 [8192, 7168], P('node'), may hold values from -0.1875 to 0.1875
Outputs:
- moe_out: bfloat16 [512, 7168], P(('group', 'node')), parts along dimension 0
The draws below stay inside these ranges and needn't reach their ends.
There are 2 independent parts, one for each index of `group`. The reference program is written for one: setup_inputs(seed, part) draws one part's arguments, and reference() takes and returns one part's arrays. A program takes and returns all parts, laid end to end along the dimension named above; an argument that names none is the same for every part. Nothing has to cross between parts.
Inputs may be any that keep to these rules, and one draw needn't show every extreme that they name: `expert_ids`: each token names 4 different experts; one expert is named by every token. `expert_place`: each slot holds exactly one expert.
All inputs are finite; a program needn't handle non-finite values.
Results may differ from the reference program's by a relative error of at most 0.005.
Values may be sent and summed in bfloat16 or wider, within the bound.
A program may use at most 128 MiB of HBM per device.

```python
import math
import jax
import jax.numpy as jnp
from jax import lax

D = 7168
FFW = 1024
EXPERTS = 8
TOP = 4
TOKENS = 256


def draw_expert_ids(key, part):
    key = jax.random.fold_in(key, 11)
    key_hot, key_popular, key_random, key_order = jax.random.split(key, 4)
    hot_expert = jax.random.randint(key_hot, (), 0, EXPERTS)
    popular = jax.random.randint(key_popular, (EXPERTS,), 0, 4) * 2 ** 18
    random_part = jax.random.randint(key_random, (TOKENS, EXPERTS), 0, 2 ** 20)
    expert_index = jnp.arange(EXPERTS, dtype=jnp.int32)
    scores = (random_part + popular[None, :]) * EXPERTS + expert_index[None, :]
    scores = jnp.where(expert_index[None, :] == hot_expert, 2 ** 30, scores)
    unused, chosen = lax.top_k(scores, TOP)
    order_scores = jax.random.randint(key_order, (TOKENS, TOP), 0, 2 ** 20) * TOP + jnp.arange(TOP, dtype=jnp.int32)[None, :]
    column_order = jnp.argsort(order_scores, axis=1, stable=True)
    return jnp.take_along_axis(chosen, column_order, axis=1).astype(jnp.int32)


def block_levels(own_key, dims, pieces, least, high):
    def one(axis_at, shards_of):
        draws = jax.random.uniform(jax.random.fold_in(jax.random.fold_in(own_key, 6), axis_at), (shards_of,), jnp.float32, least / len(pieces), high / len(pieces))
        return jnp.repeat(jnp.exp(draws), dims[axis_at] // shards_of).reshape((-1,) + (1,) * (len(dims) - axis_at - 1))

    gain = one(*pieces[0])
    for cut in pieces[1:]:
        gain = gain * one(*cut)
    return gain


def centred(stream_key, dims, width, reach, cuts=(), kind=jnp.bfloat16):
    level = block_levels(stream_key, dims, cuts, -0.22, 0.18) if cuts else 1.0
    array = jax.random.normal(stream_key, dims, jnp.float32) * width * level
    return jnp.minimum(jnp.maximum(array, -reach), reach).astype(kind)


def setup_inputs(seed: int = 0, part: int = 0) -> dict:
    keys = jax.random.split(jax.random.key(seed), 8)
    part_keys = jax.random.split(jax.random.fold_in(keys[7], part), 8)
    return {
        "tokens": centred(part_keys[0], (TOKENS, D), 1.0, 6.0, ((0, 16),)),
        "expert_ids": draw_expert_ids(jax.random.fold_in(jax.random.fold_in(keys[7], part), 71), part),
        "gates": jnp.clip(jnp.exp(math.log(1.0) - 2.306499 * jax.random.uniform(part_keys[2], (TOKENS, TOP), jnp.float32) ** block_levels(part_keys[2], (TOKENS, TOP), ((0, 16),), -0.2, 0.2)), 0.099609375, 1.0).astype(jnp.bfloat16),
        "expert_place": jax.random.permutation(keys[3], EXPERTS).astype(jnp.int32),
        "gate_proj": centred(keys[4], (D, EXPERTS * FFW), D ** -0.5, 0.0625, ((1, 16),)),
        "up_proj": centred(keys[5], (D, EXPERTS * FFW), D ** -0.5, 0.0625, ((1, 16),)),
        "down_proj": centred(keys[6], (EXPERTS * FFW, D), FFW ** -0.5, 0.1875, ((0, 16),)),
    }


def expert_rows(inputs, w_gate, w_up, w_down):
    gate_part = jnp.dot(inputs, w_gate, preferred_element_type=jnp.float32)
    up_part = jnp.dot(inputs, w_up, preferred_element_type=jnp.float32)
    hidden = (jax.nn.silu(gate_part) * up_part).astype(jnp.bfloat16)
    return jnp.dot(hidden, w_down, preferred_element_type=jnp.float32)


def reference(tokens, expert_ids, gates, expert_place, gate_proj, up_proj, down_proj):
    slot_of = expert_place[expert_ids]
    slot_range = jnp.arange(EXPERTS, dtype=jnp.int32)
    chosen = slot_of[:, :, None] == slot_range[None, None, :]
    weight_tab = jnp.sum(jnp.where(chosen, gates.astype(jnp.float32)[:, :, None], jnp.float32(0.0)), axis=1)

    def add_slot(slot_index, total):
        first_col = (slot_index * FFW).astype(jnp.int32)
        w_gate = lax.dynamic_slice_in_dim(gate_proj, first_col, FFW, 1)
        w_up = lax.dynamic_slice_in_dim(up_proj, first_col, FFW, 1)
        w_down = lax.dynamic_slice_in_dim(down_proj, first_col, FFW, 0)
        partial_value = expert_rows(tokens, w_gate, w_up, w_down)
        scale = lax.dynamic_slice_in_dim(weight_tab, slot_index.astype(jnp.int32), 1, 1)
        return total + scale * partial_value

    total = lax.fori_loop(0, EXPERTS, add_slot, jnp.zeros(tokens.shape, jnp.float32))
    return total.astype(jnp.bfloat16)
```

```python
import functools

import jax
import jax.numpy as jnp
from jax import lax
from jax.experimental import pallas as pl
from jax.experimental.pallas import tpu as pltpu
from jax.sharding import PartitionSpec as P

LANES = 128
F32 = jnp.float32
BF16 = jnp.bfloat16


def kernel(
    Z, C,
    place_ref, ids_ref, gates_ref, tokens_ref, wg_hbm, wu_hbm, wd_hbm, out_ref,
    tok, wg, wu, wd, gate_acc, up_acc, hid, own, core_out, core_in, y_out, y_in, z_out, z_in,
    tok_sem, wg_sem, wu_sem, wd_sem,
    az_s, az_r, ay_s, ay_r, ac_s, ac_r,
    rc_s, rc_r, ry_s, ry_r, rz_s, rz_r,
):
    rows, width = tokens_ref.shape
    experts = place_ref.shape[0]
    chunk = width // C
    me = lax.axis_index("node")
    core = lax.rem(me, 2)
    y = lax.rem(me // 2, 2)
    z = me // 4
    core_peer = (z * 2 + y) * 2 + 1 - core
    y_peer = (z * 2 + 1 - y) * 2 + core
    z_peer = [None] + [(lax.rem(z + d, Z) * 2 + y) * 2 + core for d in range(1, Z)]
    quarter = Z * rows
    half = 2 * quarter

    load_tok = pltpu.make_async_copy(tokens_ref, tok.at[0:rows, 0:width], tok_sem)
    load_tok.start()

    barrier = pltpu.get_barrier_semaphore()
    for peer in z_peer[1:] + [y_peer, core_peer]:
        pl.semaphore_signal(barrier, inc=1, device_id={"node": peer})

    ids = ids_ref[...]
    slot_of = jnp.zeros_like(ids)
    for e in range(experts):
        slot_of = slot_of + jnp.where(ids == e, place_ref[e], 0)
    gates = gates_ref[...].astype(F32)
    lane = lax.broadcasted_iota(jnp.int32, (rows, LANES), 1)
    table = jnp.zeros((rows, LANES), F32)
    for k in range(ids.shape[1]):
        table = table + jnp.where(slot_of[:, k:k + 1] == lane, gates[:, k:k + 1], 0.0)
    tok[0:rows, width:width + LANES] = table.astype(BF16)

    def cols(c):
        return pl.ds(c * chunk, chunk)

    def cols_tab(c):
        return pl.ds(c * chunk, chunk + (LANES if c == C - 1 else 0))

    def remote(src, dst, send, recv, peer):
        return pltpu.make_async_remote_copy(
            src_ref=src, dst_ref=dst, send_sem=send, recv_sem=recv,
            device_id={"node": peer}, device_id_type=pl.DeviceIdType.MESH,
        )

    load_tok.wait()
    pl.semaphore_wait(barrier, Z + 1)

    gz, gy, gc = [], [], []
    for c in range(C):
        own_block = tok.at[0:rows, cols_tab(c)]
        gz.append([
            remote(own_block, tok.at[(Z - d) * rows:(Z - d + 1) * rows, cols_tab(c)],
                   az_s.at[c, d], az_r.at[c, Z - d], z_peer[d])
            for d in range(1, Z)
        ])
        gy.append(remote(tok.at[0:quarter, cols_tab(c)], tok.at[quarter:half, cols_tab(c)],
                         ay_s.at[c], ay_r.at[c], y_peer))
        gc.append([
            remote(tok.at[h * quarter:(h + 1) * quarter, cols_tab(c)],
                   tok.at[half + h * quarter:half + (h + 1) * quarter, cols_tab(c)],
                   ac_s.at[c, h], ac_r.at[c, h], core_peer)
            for h in range(2)
        ])
    for c in range(C):
        for copy in gz[c]:
            copy.start()
    loads = []
    for c in range(C):
        loads.append([
            pltpu.make_async_copy(wg_hbm.at[cols(c), :], wg.at[cols(c), :], wg_sem.at[c]),
            pltpu.make_async_copy(wu_hbm.at[cols(c), :], wu.at[cols(c), :], wu_sem.at[c]),
        ])
        for copy in loads[c]:
            copy.start()
    load_down = [
        pltpu.make_async_copy(wd_hbm.at[:, cols(c)], wd.at[:, cols(c)], wd_sem.at[c])
        for c in range(C)
    ]
    for copy in load_down:
        copy.start()

    for step in range(C + 2):
        if step < C:
            c = step
            for copy in gz[c]:
                copy.wait_recv()
            gy[c].start()
            gc[c][0].start()
        if 0 <= step - 1 < C:
            c = step - 1
            gy[c].wait_recv()
            gc[c][1].start()
        if 0 <= step - 2 < C:
            c = step - 2
            for copy in loads[c]:
                copy.wait()
            for copy in gc[c]:
                copy.wait_recv()
            x = tok[:, cols(c)]
            gate_part = jnp.dot(x, wg[cols(c), :], preferred_element_type=F32)
            up_part = jnp.dot(x, wu[cols(c), :], preferred_element_type=F32)
            if c == 0:
                gate_acc[...] = gate_part
                up_acc[...] = up_part
            elif c < C - 1:
                gate_acc[...] += gate_part
                up_acc[...] += up_part
            else:
                gate_part = gate_acc[...] + gate_part
                up_part = up_acc[...] + up_part
                hid[...] = (jax.nn.silu(gate_part) * up_part).astype(BF16)

    all_rows = 2 * half
    lane = lax.broadcasted_iota(jnp.int32, (all_rows, LANES), 1)
    scale = jnp.sum(
        jnp.where(lane == me // 2, tok[:, width:width + LANES].astype(F32), 0.0),
        axis=1, keepdims=True,
    )

    sc = [remote(core_out.at[:, cols(c)], core_in.at[:, cols(c)], rc_s.at[c], rc_r.at[c], core_peer)
          for c in range(C)]
    sy = [remote(y_out.at[:, cols(c)], y_in.at[:, cols(c)], ry_s.at[c], ry_r.at[c], y_peer)
          for c in range(C)]
    sz = [[remote(z_out.at[d * rows:(d + 1) * rows, cols(c)],
                  z_in.at[(Z - d) * rows:(Z - d + 1) * rows, cols(c)],
                  rz_s.at[c, d], rz_r.at[c, Z - d], z_peer[d]) for d in range(1, Z)]
          for c in range(C)]

    for step in range(C + 3):
        if step < C:
            c = step
            load_down[c].wait()
            part = scale * jnp.dot(hid[...], wd[:, cols(c)], preferred_element_type=F32)
            core_out[:, cols(c)] = part[half:].astype(BF16)
            sc[c].start()
            own[:, cols(c)] = part[:half]
        if 0 <= step - 1 < C:
            c = step - 1
            sc[c].wait_recv()
            total = own[:, cols(c)] + core_in[:, cols(c)].astype(F32)
            y_out[:, cols(c)] = total[quarter:].astype(BF16)
            sy[c].start()
            own[0:quarter, cols(c)] = total[:quarter]
        if 0 <= step - 2 < C:
            c = step - 2
            sy[c].wait_recv()
            total = own[0:quarter, cols(c)] + y_in[:, cols(c)].astype(F32)
            z_out[rows:, cols(c)] = total[rows:].astype(BF16)
            for copy in sz[c]:
                copy.start()
            own[0:rows, cols(c)] = total[:rows]
        if 0 <= step - 3 < C:
            c = step - 3
            for copy in sz[c]:
                copy.wait_recv()
            total = own[0:rows, cols(c)]
            for d in range(1, Z):
                total = total + z_in[d * rows:(d + 1) * rows, cols(c)].astype(F32)
            out_ref[:, cols(c)] = total.astype(BF16)

    for c in range(C):
        for copy in gz[c] + [gy[c]] + gc[c] + [sc[c], sy[c]] + sz[c]:
            copy.wait_send()


def per_device(tokens, expert_ids, gates, expert_place, gate_proj, up_proj, down_proj):
    nodes = lax.axis_size("node")
    Z = nodes // 4
    C = 7
    rows, width = tokens.shape
    units = gate_proj.shape[1]
    all_rows = nodes * rows
    dma = pltpu.SemaphoreType.DMA
    vmem = pl.BlockSpec(memory_space=pltpu.VMEM)
    hbm = pl.BlockSpec(memory_space=pl.ANY)
    return pl.pallas_call(
        functools.partial(kernel, Z, C),
        out_shape=jax.ShapeDtypeStruct((rows, width), BF16),
        in_specs=[pl.BlockSpec(memory_space=pltpu.SMEM), vmem, vmem, hbm, hbm, hbm, hbm],
        out_specs=vmem,
        scratch_shapes=[
            pltpu.VMEM((all_rows, width + LANES), BF16),
            pltpu.VMEM((width, units), BF16),
            pltpu.VMEM((width, units), BF16),
            pltpu.VMEM((units, width), BF16),
            pltpu.VMEM((all_rows, units), F32),
            pltpu.VMEM((all_rows, units), F32),
            pltpu.VMEM((all_rows, units), BF16),
            pltpu.VMEM((all_rows // 2, width), F32),
            pltpu.VMEM((all_rows // 2, width), BF16),
            pltpu.VMEM((all_rows // 2, width), BF16),
            pltpu.VMEM((all_rows // 4, width), BF16),
            pltpu.VMEM((all_rows // 4, width), BF16),
            pltpu.VMEM((all_rows // 4, width), BF16),
            pltpu.VMEM((all_rows // 4, width), BF16),
            dma, dma((C,)), dma((C,)), dma((C,)),
            dma((C, Z)), dma((C, Z)), dma((C,)), dma((C,)), dma((C, 2)), dma((C, 2)),
            dma((C,)), dma((C,)), dma((C,)), dma((C,)), dma((C, Z)), dma((C, Z)),
        ],
        compiler_params=pltpu.CompilerParams(
            collective_id=0, has_side_effects=True, vmem_limit_bytes=60 * 2 ** 20
        ),
        cost_estimate=pl.CostEstimate(
            flops=6 * all_rows * width * units,
            bytes_accessed=6 * width * units,
            transcendentals=all_rows * units,
        ),
    )(expert_place, expert_ids, gates, tokens, gate_proj, up_proj, down_proj)


def solution(mesh):
    placed = (
        P(("group", "node"), None),
        P(("group", "node"), None),
        P(("group", "node"), None),
        P(),
        P(None, "node"),
        P(None, "node"),
        P("node", None),
    )
    return jax.shard_map(
        per_device,
        mesh=mesh,
        in_specs=placed,
        out_specs=P(("group", "node"), None),
        check_vma=False,
    )
```

```python
import functools

import jax
import jax.numpy as jnp
from jax import lax
from jax.experimental import pallas as pl
from jax.experimental.pallas import tpu as pltpu
from jax.sharding import PartitionSpec as P

LANES = 128
F32 = jnp.float32
BF16 = jnp.bfloat16


def kernel(
    Z, C,
    place_ref, ids_ref, gates_ref, tokens_ref, wg_hbm, wu_hbm, wd_hbm, out_ref,
    tok, wg, wu, wd, gate_acc, up_acc, hid, own, core_out, core_in, y_out, y_in, z_out, z_in,
    tok_sem, wg_sem, wu_sem, wd_sem,
    az_s, az_r, ao_s, ao_r, ay_s, ay_r, ac_s, ac_r,
    rc_s, rc_r, ro_s, ro_r, ry_s, ry_r, rz_s, rz_r,
):
    rows, width = tokens_ref.shape
    experts = place_ref.shape[0]
    chunk = width // C
    me = lax.axis_index("node")
    core = lax.rem(me, 2)
    y = lax.rem(me // 2, 2)
    z = me // 4
    core_peer = (z * 2 + y) * 2 + 1 - core
    y_peer = (z * 2 + 1 - y) * 2 + core
    z_peer = [None] + [(lax.rem(z + d, Z) * 2 + y) * 2 + core for d in range(1, Z)]
    quarter = Z * rows
    half = 2 * quarter

    load_tok = pltpu.make_async_copy(tokens_ref, tok.at[0:rows, 0:width], tok_sem)
    load_tok.start()

    barrier = pltpu.get_barrier_semaphore()
    for peer in z_peer[1:] + [y_peer, core_peer]:
        pl.semaphore_signal(barrier, inc=1, device_id={"node": peer})

    def cols(c):
        return pl.ds(c * chunk, chunk)

    def cols_tab(c):
        return pl.ds(c * chunk, chunk + (LANES if c == C - 1 else 0))

    def remote(src, dst, send, recv, peer):
        return pltpu.make_async_remote_copy(
            src_ref=src, dst_ref=dst, send_sem=send, recv_sem=recv,
            device_id={"node": peer}, device_id_type=pl.DeviceIdType.MESH,
        )

    load_tok.wait()
    pl.semaphore_wait(barrier, Z + 1)

    gz, go, gy, gc = [], [], [], []
    for c in range(C):
        own_block = tok.at[0:rows, cols_tab(c)]
        gz.append([
            remote(own_block, tok.at[(Z - d) * rows:(Z - d + 1) * rows, cols_tab(c)],
                   az_s.at[c, d], az_r.at[c, Z - d], z_peer[d])
            for d in range(1, Z)
        ])
        go.append(remote(own_block, tok.at[quarter:quarter + rows, cols_tab(c)],
                         ao_s.at[c], ao_r.at[c], y_peer))
        gy.append(remote(tok.at[rows:quarter, cols_tab(c)],
                         tok.at[quarter + rows:half, cols_tab(c)],
                         ay_s.at[c], ay_r.at[c], y_peer))
        gc.append([
            remote(tok.at[h * quarter:(h + 1) * quarter, cols_tab(c)],
                   tok.at[half + h * quarter:half + (h + 1) * quarter, cols_tab(c)],
                   ac_s.at[c, h], ac_r.at[c, h], core_peer)
            for h in range(2)
        ])
    for c in range(2):
        for copy in gz[c] + [go[c]]:
            copy.start()
    for c in range(2, C - 1):
        go[c].start()
    loads = []
    for c in range(C):
        loads.append([
            pltpu.make_async_copy(wg_hbm.at[cols(c), :], wg.at[cols(c), :], wg_sem.at[c]),
            pltpu.make_async_copy(wu_hbm.at[cols(c), :], wu.at[cols(c), :], wu_sem.at[c]),
        ])
        for copy in loads[c]:
            copy.start()
    load_down = [
        pltpu.make_async_copy(wd_hbm.at[:, cols(c)], wd.at[:, cols(c)], wd_sem.at[c])
        for c in range(C)
    ]
    for copy in load_down:
        copy.start()

    ids = ids_ref[...]
    slot_of = jnp.zeros_like(ids)
    for e in range(experts):
        slot_of = slot_of + jnp.where(ids == e, place_ref[e], 0)
    gates = gates_ref[...].astype(F32)
    slot = lax.broadcasted_iota(jnp.int32, (LANES, rows), 0)
    table = jnp.zeros((LANES, rows), F32)
    for k in range(ids.shape[0]):
        table = table + jnp.where(slot_of[k:k + 1, :] == slot, gates[k:k + 1, :], 0.0)
    tok[0:rows, width:width + LANES] = table.T.astype(BF16)
    go[C - 1].start()

    for step in range(C + 2):
        if step < C:
            c = step
            for copy in gz[c]:
                copy.wait_recv()
            gy[c].start()
            gc[c][0].start()
            if c + 2 < C:
                for copy in gz[c + 2]:
                    copy.start()
        if 0 <= step - 1 < C:
            c = step - 1
            go[c].wait_recv()
            gy[c].wait_recv()
            gc[c][1].start()
        if 0 <= step - 2 < C:
            c = step - 2
            for copy in loads[c]:
                copy.wait()
            for copy in gc[c]:
                copy.wait_recv()
            x = tok[:, cols(c)]
            gate_part = jnp.dot(x, wg[cols(c), :], preferred_element_type=F32)
            up_part = jnp.dot(x, wu[cols(c), :], preferred_element_type=F32)
            if c == 0:
                gate_acc[...] = gate_part
                up_acc[...] = up_part
            elif c < C - 1:
                gate_acc[...] += gate_part
                up_acc[...] += up_part
            else:
                gate_part = gate_acc[...] + gate_part
                up_part = up_acc[...] + up_part
                hid[...] = (jax.nn.silu(gate_part) * up_part).astype(BF16)

    all_rows = 2 * half
    lane = lax.broadcasted_iota(jnp.int32, (all_rows, LANES), 1)
    scale = jnp.sum(
        jnp.where(lane == me // 2, tok[:, width:width + LANES].astype(F32), 0.0),
        axis=1, keepdims=True,
    )

    sc = [remote(core_out.at[:, cols(c)], core_in.at[:, cols(c)], rc_s.at[c], rc_r.at[c], core_peer)
          for c in range(C)]
    so = [remote(y_out.at[0:rows, cols(c)], y_in.at[0:rows, cols(c)],
                 ro_s.at[c], ro_r.at[c], y_peer) for c in range(C)]
    sy = [remote(y_out.at[rows:quarter, cols(c)], y_in.at[rows:quarter, cols(c)],
                 ry_s.at[c], ry_r.at[c], y_peer) for c in range(C)]
    sz = [[remote(z_out.at[d * rows:(d + 1) * rows, cols(c)],
                  z_in.at[(Z - d) * rows:(Z - d + 1) * rows, cols(c)],
                  rz_s.at[c, d], rz_r.at[c, Z - d], z_peer[d]) for d in range(1, Z)]
          for c in range(C)]

    for step in range(C + 2):
        if step < C:
            c = step
            load_down[c].wait()
            part = scale * jnp.dot(hid[...], wd[:, cols(c)], preferred_element_type=F32)
            core_out[:, cols(c)] = part[half:].astype(BF16)
            sc[c].start()
            own[:, cols(c)] = part[:half]
        if 0 <= step - 1 < C:
            c = step - 1
            sc[c].wait_recv()
            total = own[:, cols(c)] + core_in[:, cols(c)].astype(F32)
            y_out[:, cols(c)] = total[quarter:].astype(BF16)
            sy[c].start()
            own[0:quarter, cols(c)] = total[:quarter]
            if c == C - 1:
                for copy in so:
                    copy.start()
        if 0 <= step - 2 < C:
            c = step - 2
            sy[c].wait_recv()
            total = own[rows:quarter, cols(c)] + y_in[rows:, cols(c)].astype(F32)
            z_out[rows:, cols(c)] = total.astype(BF16)
            for copy in sz[c]:
                copy.start()
    for c in range(C):
        so[c].wait_recv()
        for copy in sz[c]:
            copy.wait_recv()
        total = own[0:rows, cols(c)] + y_in[0:rows, cols(c)].astype(F32)
        for d in range(1, Z):
            total = total + z_in[d * rows:(d + 1) * rows, cols(c)].astype(F32)
        out_ref[:, cols(c)] = total.astype(BF16)

    for c in range(C):
        for copy in gz[c] + [go[c], gy[c]] + gc[c] + [sc[c], so[c], sy[c]] + sz[c]:
            copy.wait_send()


def per_device(tokens, expert_ids, gates, expert_place, gate_proj, up_proj, down_proj):
    nodes = lax.axis_size("node")
    Z = nodes // 4
    C = 7
    rows, width = tokens.shape
    units = gate_proj.shape[1]
    all_rows = nodes * rows
    dma = pltpu.SemaphoreType.DMA
    vmem = pl.BlockSpec(memory_space=pltpu.VMEM)
    hbm = pl.BlockSpec(memory_space=pl.ANY)
    return pl.pallas_call(
        functools.partial(kernel, Z, C),
        out_shape=jax.ShapeDtypeStruct((rows, width), BF16),
        in_specs=[pl.BlockSpec(memory_space=pltpu.SMEM), vmem, vmem, hbm, hbm, hbm, hbm],
        out_specs=vmem,
        scratch_shapes=[
            pltpu.VMEM((all_rows, width + LANES), BF16),
            pltpu.VMEM((width, units), BF16),
            pltpu.VMEM((width, units), BF16),
            pltpu.VMEM((units, width), BF16),
            pltpu.VMEM((all_rows, units), F32),
            pltpu.VMEM((all_rows, units), F32),
            pltpu.VMEM((all_rows, units), BF16),
            pltpu.VMEM((all_rows // 2, width), F32),
            pltpu.VMEM((all_rows // 2, width), BF16),
            pltpu.VMEM((all_rows // 2, width), BF16),
            pltpu.VMEM((all_rows // 4, width), BF16),
            pltpu.VMEM((all_rows // 4, width), BF16),
            pltpu.VMEM((all_rows // 4, width), BF16),
            pltpu.VMEM((all_rows // 4, width), BF16),
            dma, dma((C,)), dma((C,)), dma((C,)),
            dma((C, Z)), dma((C, Z)), dma((C,)), dma((C,)), dma((C,)), dma((C,)), dma((C, 2)), dma((C, 2)),
            dma((C,)), dma((C,)), dma((C,)), dma((C,)), dma((C,)), dma((C,)), dma((C, Z)), dma((C, Z)),
        ],
        compiler_params=pltpu.CompilerParams(
            collective_id=0, has_side_effects=True, vmem_limit_bytes=60 * 2 ** 20
        ),
        cost_estimate=pl.CostEstimate(
            flops=6 * all_rows * width * units,
            bytes_accessed=6 * width * units,
            transcendentals=all_rows * units,
        ),
    )(expert_place, expert_ids.T, gates.T, tokens, gate_proj, up_proj, down_proj)


def solution(mesh):
    placed = (
        P(("group", "node"), None),
        P(("group", "node"), None),
        P(("group", "node"), None),
        P(),
        P(None, "node"),
        P(None, "node"),
        P("node", None),
    )
    return jax.shard_map(
        per_device,
        mesh=mesh,
        in_specs=placed,
        out_specs=P(("group", "node"), None),
        check_vma=False,
    )
```

```python
import functools

import jax
import jax.numpy as jnp
from jax import lax
from jax.experimental import pallas as pl
from jax.experimental.pallas import tpu as pltpu
from jax.sharding import PartitionSpec as P

LANES = 128
F32 = jnp.float32
BF16 = jnp.bfloat16


def kernel(
    Z, C,
    place_ref, ids_ref, gates_ref, tokens_ref, wg_hbm, wu_hbm, wd_hbm, out_ref,
    tok, wg, wu, wd, gate_acc, up_acc, hid, own, core_out, core_in, y_out, y_in, z_out, z_in,
    tok_sem, wg_sem, wu_sem, wd_sem,
    az_s, az_r, al_s, ao_s, ao_r, ay_s, ay_r, ac_s, ac_r,
    rc_s, rc_r, ro_s, ro_r, ry_s, ry_r, rz_s, rz_r,
):
    rows, width = tokens_ref.shape
    experts = place_ref.shape[0]
    chunk = width // C
    me = lax.axis_index("node")
    core = lax.rem(me, 2)
    y = lax.rem(me // 2, 2)
    z = me // 4
    core_peer = (z * 2 + y) * 2 + 1 - core
    y_peer = (z * 2 + 1 - y) * 2 + core
    z_peer = [None] + [(lax.rem(z + d, Z) * 2 + y) * 2 + core for d in range(1, Z)]
    quarter = Z * rows
    half = 2 * quarter

    load_tok = pltpu.make_async_copy(tokens_ref, tok.at[0:rows, 0:width], tok_sem)
    load_tok.start()

    barrier = pltpu.get_barrier_semaphore()
    for peer in z_peer[1:] + [y_peer, core_peer]:
        pl.semaphore_signal(barrier, inc=1, device_id={"node": peer})

    def cols(c):
        return pl.ds(c * chunk, chunk)

    def cols_tab(c):
        return pl.ds(c * chunk, chunk + (LANES if c == C - 1 else 0))

    def remote(src, dst, send, recv, peer):
        return pltpu.make_async_remote_copy(
            src_ref=src, dst_ref=dst, send_sem=send, recv_sem=recv,
            device_id={"node": peer}, device_id_type=pl.DeviceIdType.MESH,
        )

    load_tok.wait()
    pl.semaphore_wait(barrier, Z + 1)

    gz, go, gy, gc = [], [], [], []
    for c in range(C):
        own_block = tok.at[0:rows, cols_tab(c)]
        gz.append([
            remote(own_block, tok.at[(Z - d) * rows:(Z - d + 1) * rows, cols_tab(c)],
                   az_s.at[c, d], az_r.at[c, Z - d], z_peer[d])
            for d in range(1, Z)
        ])
        gy.append(remote(tok.at[rows:quarter, cols_tab(c)],
                         tok.at[quarter + rows:half, cols_tab(c)],
                         ay_s.at[c], ay_r.at[c], y_peer))
        gc.append(remote(tok.at[0:half, cols_tab(c)], tok.at[half:2 * half, cols_tab(c)],
                         ac_s.at[c], ac_r.at[c], core_peer))
    split = C // 2 + 1
    for g, span in enumerate([
        pl.ds(0, split * chunk), pl.ds(split * chunk, (C - split) * chunk + LANES)
    ]):
        go.append(remote(tok.at[0:rows, span], tok.at[quarter:quarter + rows, span],
                         ao_s.at[g], ao_r.at[g], y_peer))
    relayed = Z == 4
    relay = [
        (remote(tok.at[2 * rows:3 * rows, cols_tab(c)], tok.at[3 * rows:4 * rows, cols_tab(c)],
                al_s.at[c], az_r.at[c, 3], z_peer[3]),
         remote(tok.at[2 * rows:3 * rows, cols_tab(c)], tok.at[rows:2 * rows, cols_tab(c)],
                al_s.at[c], az_r.at[c, 1], z_peer[1]))
        for c in range(C)
    ] if relayed else []

    def each_z(c, act):
        for d in [2, 1] + list(range(3, Z)):
            if relayed and d != 2:
                pl.when(z != (3 if d == 1 else 0))(functools.partial(act, gz[c][d - 1]))
            else:
                act(gz[c][d - 1])

    def each_relay(c, act):
        for at, copy in enumerate(relay[c] if relayed else ()):
            pl.when(z == at + 1)(functools.partial(act, copy))

    def start(copy):
        copy.start()

    def wait_send(copy):
        copy.wait_send()

    each_z(0, start)
    go[0].start()
    for c in range(1, 3):
        each_z(c, start)
    loads = []
    for c in range(C):
        loads.append([
            pltpu.make_async_copy(wg_hbm.at[cols(c), :], wg.at[cols(c), :], wg_sem.at[c]),
            pltpu.make_async_copy(wu_hbm.at[cols(c), :], wu.at[cols(c), :], wu_sem.at[c]),
        ])
        for copy in loads[c]:
            copy.start()
    load_down = [
        pltpu.make_async_copy(wd_hbm.at[:, cols(c)], wd.at[:, cols(c)], wd_sem.at[c])
        for c in range(C)
    ]
    for copy in load_down:
        copy.start()

    ids = ids_ref[...]
    slot_of = jnp.zeros_like(ids)
    for e in range(experts):
        slot_of = slot_of + jnp.where(ids == e, place_ref[e], 0)
    gates = gates_ref[...].astype(F32)
    slot = lax.broadcasted_iota(jnp.int32, (LANES, rows), 0)
    table = jnp.zeros((LANES, rows), F32)
    for k in range(ids.shape[0]):
        table = table + jnp.where(slot_of[k:k + 1, :] == slot, gates[k:k + 1, :], 0.0)
    tok[0:rows, width:width + LANES] = table.T.astype(BF16)
    go[1].start()

    for step in range(C + 2):
        if step < C:
            c = step
            gz[c][1].wait_recv()
            each_relay(c, start)
            for copy in gz[c][0:1] + gz[c][2:]:
                copy.wait_recv()
            gy[c].start()
            if c + 3 < C:
                each_z(c + 3, start)
        if 0 <= step - 1 < C:
            c = step - 1
            if c in (0, split):
                go[c // split].wait_recv()
            gy[c].wait_recv()
            gc[c].start()
        if 0 <= step - 2 < C:
            c = step - 2
            for copy in loads[c]:
                copy.wait()
            gc[c].wait_recv()
            x = tok[:, cols(c)]
            gate_part = jnp.dot(x, wg[cols(c), :], preferred_element_type=F32)
            up_part = jnp.dot(x, wu[cols(c), :], preferred_element_type=F32)
            if c == 0:
                gate_acc[...] = gate_part
                up_acc[...] = up_part
            elif c < C - 1:
                gate_acc[...] += gate_part
                up_acc[...] += up_part
            else:
                gate_part = gate_acc[...] + gate_part
                up_part = up_acc[...] + up_part
                hid[...] = (jax.nn.silu(gate_part) * up_part).astype(BF16)

    all_rows = 2 * half
    lane = lax.broadcasted_iota(jnp.int32, (all_rows, LANES), 1)
    scale = jnp.sum(
        jnp.where(lane == me // 2, tok[:, width:width + LANES].astype(F32), 0.0),
        axis=1, keepdims=True,
    )

    sc = [remote(core_out.at[:, cols(c)], core_in.at[:, cols(c)], rc_s.at[c], rc_r.at[c], core_peer)
          for c in range(C)]
    so = [remote(y_out.at[0:rows, span], y_in.at[0:rows, span], ro_s.at[g], ro_r.at[g], y_peer)
          for g, span in enumerate([
              pl.ds(0, split * chunk), pl.ds(split * chunk, (C - split) * chunk)
          ])]
    sy = [remote(y_out.at[rows:quarter, cols(c)], y_in.at[rows:quarter, cols(c)],
                 ry_s.at[c], ry_r.at[c], y_peer) for c in range(C)]
    sz = [[remote(z_out.at[d * rows:(d + 1) * rows, cols(c)],
                  z_in.at[(Z - d) * rows:(Z - d + 1) * rows, cols(c)],
                  rz_s.at[c, d], rz_r.at[c, Z - d], z_peer[d]) for d in range(1, Z)]
          for c in range(C)]

    for step in range(C + 2):
        if step < C:
            c = step
            load_down[c].wait()
            part = scale * jnp.dot(hid[...], wd[:, cols(c)], preferred_element_type=F32)
            core_out[:, cols(c)] = part[half:].astype(BF16)
            sc[c].start()
            own[:, cols(c)] = part[:half]
        if 0 <= step - 1 < C:
            c = step - 1
            sc[c].wait_recv()
            total = own[:, cols(c)] + core_in[:, cols(c)].astype(F32)
            y_out[:, cols(c)] = total[quarter:].astype(BF16)
            sy[c].start()
            own[0:quarter, cols(c)] = total[:quarter]
            if c == C - 1:
                for copy in so:
                    copy.start()
        if 0 <= step - 2 < C:
            c = step - 2
            sy[c].wait_recv()
            total = own[rows:quarter, cols(c)] + y_in[rows:, cols(c)].astype(F32)
            z_out[rows:, cols(c)] = total.astype(BF16)
            for copy in sz[c]:
                copy.start()
    for c in range(C):
        if c in (0, split):
            so[c // split].wait_recv()
        for copy in sz[c]:
            copy.wait_recv()
        total = own[0:rows, cols(c)] + y_in[0:rows, cols(c)].astype(F32)
        for d in range(1, Z):
            total = total + z_in[d * rows:(d + 1) * rows, cols(c)].astype(F32)
        out_ref[:, cols(c)] = total.astype(BF16)

    for c in range(C):
        each_z(c, wait_send)
        each_relay(c, wait_send)
        for copy in [gy[c], gc[c], sc[c], sy[c]] + sz[c]:
            copy.wait_send()
    for copy in go + so:
        copy.wait_send()


def per_device(tokens, expert_ids, gates, expert_place, gate_proj, up_proj, down_proj):
    nodes = lax.axis_size("node")
    Z = nodes // 4
    C = 7
    rows, width = tokens.shape
    units = gate_proj.shape[1]
    all_rows = nodes * rows
    dma = pltpu.SemaphoreType.DMA
    vmem = pl.BlockSpec(memory_space=pltpu.VMEM)
    hbm = pl.BlockSpec(memory_space=pl.ANY)
    return pl.pallas_call(
        functools.partial(kernel, Z, C),
        out_shape=jax.ShapeDtypeStruct((rows, width), BF16),
        in_specs=[pl.BlockSpec(memory_space=pltpu.SMEM), vmem, vmem, hbm, hbm, hbm, hbm],
        out_specs=vmem,
        scratch_shapes=[
            pltpu.VMEM((all_rows, width + LANES), BF16),
            pltpu.VMEM((width, units), BF16),
            pltpu.VMEM((width, units), BF16),
            pltpu.VMEM((units, width), BF16),
            pltpu.VMEM((all_rows, units), F32),
            pltpu.VMEM((all_rows, units), F32),
            pltpu.VMEM((all_rows, units), BF16),
            pltpu.VMEM((all_rows // 2, width), F32),
            pltpu.VMEM((all_rows // 2, width), BF16),
            pltpu.VMEM((all_rows // 2, width), BF16),
            pltpu.VMEM((all_rows // 4, width), BF16),
            pltpu.VMEM((all_rows // 4, width), BF16),
            pltpu.VMEM((all_rows // 4, width), BF16),
            pltpu.VMEM((all_rows // 4, width), BF16),
            dma, dma((C,)), dma((C,)), dma((C,)),
            dma((C, Z)), dma((C, Z)), dma((C,)), dma((2,)), dma((2,)),
            dma((C,)), dma((C,)), dma((C,)), dma((C,)),
            dma((C,)), dma((C,)), dma((2,)), dma((2,)), dma((C,)), dma((C,)), dma((C, Z)), dma((C, Z)),
        ],
        compiler_params=pltpu.CompilerParams(
            collective_id=0, has_side_effects=True, vmem_limit_bytes=60 * 2 ** 20
        ),
        cost_estimate=pl.CostEstimate(
            flops=6 * all_rows * width * units,
            bytes_accessed=6 * width * units,
            transcendentals=all_rows * units,
        ),
    )(expert_place, expert_ids.T, gates.T, tokens, gate_proj, up_proj, down_proj)


def solution(mesh):
    placed = (
        P(("group", "node"), None),
        P(("group", "node"), None),
        P(("group", "node"), None),
        P(),
        P(None, "node"),
        P(None, "node"),
        P("node", None),
    )
    return jax.shard_map(
        per_device,
        mesh=mesh,
        in_specs=placed,
        out_specs=P(("group", "node"), None),
        check_vma=False,
    )
```

```python
import functools

import jax
import jax.numpy as jnp
from jax import lax
from jax.experimental import pallas as pl
from jax.experimental.pallas import tpu as pltpu
from jax.sharding import PartitionSpec as P

LANES = 128
F32 = jnp.float32
BF16 = jnp.bfloat16


def kernel(
    Z, C,
    place_ref, ids_ref, gates_ref, tokens_ref, wg_hbm, wu_hbm, wd_hbm, out_ref,
    tok, wg, wu, wd, gate_acc, up_acc, hid, own, core_out, core_in, y_out, y_in, z_out, z_in,
    tok_sem, wg_sem, wu_sem, wd_sem,
    az_s, az_r, al_s, ao_s, ao_r, ay_s, ay_r, ac_s, ac_r,
    rc_s, rc_r, ro_s, ro_r, ry_s, ry_r, rz_s, rz_r,
):
    rows, width = tokens_ref.shape
    experts = place_ref.shape[0]
    chunk = width // C
    me = lax.axis_index("node")
    core = lax.rem(me, 2)
    y = lax.rem(me // 2, 2)
    z = me // 4
    core_peer = (z * 2 + y) * 2 + 1 - core
    y_peer = (z * 2 + 1 - y) * 2 + core
    z_peer = [None] + [(lax.rem(z + d, Z) * 2 + y) * 2 + core for d in range(1, Z)]
    quarter = Z * rows
    half = 2 * quarter

    load_tok = pltpu.make_async_copy(tokens_ref, tok.at[0:rows, 0:width], tok_sem)
    load_tok.start()

    barrier = pltpu.get_barrier_semaphore()
    for peer in z_peer[1:] + [y_peer, core_peer]:
        pl.semaphore_signal(barrier, inc=1, device_id={"node": peer})

    def cols(c):
        return pl.ds(c * chunk, chunk)

    def cols_tab(c):
        return pl.ds(c * chunk, chunk + (LANES if c == C - 1 else 0))

    def remote(src, dst, send, recv, peer):
        return pltpu.make_async_remote_copy(
            src_ref=src, dst_ref=dst, send_sem=send, recv_sem=recv,
            device_id={"node": peer}, device_id_type=pl.DeviceIdType.MESH,
        )

    load_tok.wait()
    pl.semaphore_wait(barrier, Z + 1)

    gz, go, gy, gc = [], [], [], []
    for c in range(C):
        own_block = tok.at[0:rows, cols_tab(c)]
        gz.append([
            remote(own_block, tok.at[(Z - d) * rows:(Z - d + 1) * rows, cols_tab(c)],
                   az_s.at[c, d], az_r.at[c, Z - d], z_peer[d])
            for d in range(1, Z)
        ])
        gy.append(remote(tok.at[rows:quarter, cols_tab(c)],
                         tok.at[quarter + rows:half, cols_tab(c)],
                         ay_s.at[c], ay_r.at[c], y_peer))
        gc.append(remote(tok.at[0:half, cols_tab(c)], tok.at[half:2 * half, cols_tab(c)],
                         ac_s.at[c], ac_r.at[c], core_peer))
    split = C // 2 + 1
    for g, span in enumerate([
        pl.ds(0, split * chunk), pl.ds(split * chunk, (C - split) * chunk + LANES)
    ]):
        go.append(remote(tok.at[0:rows, span], tok.at[quarter:quarter + rows, span],
                         ao_s.at[g], ao_r.at[g], y_peer))
    relayed = Z == 4
    relay = [
        (remote(tok.at[2 * rows:3 * rows, cols_tab(c)], tok.at[3 * rows:4 * rows, cols_tab(c)],
                al_s.at[c], az_r.at[c, 3], z_peer[3]),
         remote(tok.at[2 * rows:3 * rows, cols_tab(c)], tok.at[rows:2 * rows, cols_tab(c)],
                al_s.at[c], az_r.at[c, 1], z_peer[1]))
        for c in range(C)
    ] if relayed else []

    def each_z(c, act):
        for d in [2, 1] + list(range(3, Z)):
            if relayed and d != 2:
                pl.when(z != (3 if d == 1 else 0))(functools.partial(act, gz[c][d - 1]))
            else:
                act(gz[c][d - 1])

    def each_relay(c, act):
        for at, copy in enumerate(relay[c] if relayed else ()):
            pl.when(z == at + 1)(functools.partial(act, copy))

    def start(copy):
        copy.start()

    def wait_send(copy):
        copy.wait_send()

    each_z(0, start)
    go[0].start()
    for c in range(1, 3):
        each_z(c, start)
    loads = []
    for c in range(C):
        loads.append([
            pltpu.make_async_copy(wg_hbm.at[cols(c), :], wg.at[cols(c), :], wg_sem.at[c]),
            pltpu.make_async_copy(wu_hbm.at[cols(c), :], wu.at[cols(c), :], wu_sem.at[c]),
        ])
        for copy in loads[c]:
            copy.start()
    load_down = [
        pltpu.make_async_copy(wd_hbm.at[:, cols(c)], wd.at[:, cols(c)], wd_sem.at[c])
        for c in range(C)
    ]
    for copy in load_down:
        copy.start()

    ids = ids_ref[...]
    slot_of = jnp.zeros_like(ids)
    for e in range(experts):
        slot_of = slot_of + jnp.where(ids == e, place_ref[e], 0)
    gates = gates_ref[...].astype(F32)
    slot = lax.broadcasted_iota(jnp.int32, (LANES, rows), 0)
    table = jnp.zeros((LANES, rows), F32)
    for k in range(ids.shape[0]):
        table = table + jnp.where(slot_of[k:k + 1, :] == slot, gates[k:k + 1, :], 0.0)
    tok[0:rows, width:width + LANES] = table.T.astype(BF16)
    go[1].start()

    for step in range(C + 2):
        if step < C:
            c = step
            gz[c][1].wait_recv()
            each_relay(c, start)
            for copy in gz[c][0:1] + gz[c][2:]:
                copy.wait_recv()
            gy[c].start()
            if c + 3 < C:
                each_z(c + 3, start)
        if 0 <= step - 1 < C:
            c = step - 1
            if c in (0, split):
                go[c // split].wait_recv()
            gy[c].wait_recv()
            gc[c].start()
        if 0 <= step - 2 < C:
            c = step - 2
            for copy in loads[c]:
                copy.wait()
            gc[c].wait_recv()
            x = tok[:, cols(c)]
            gate_part = jnp.dot(x, wg[cols(c), :], preferred_element_type=F32)
            up_part = jnp.dot(x, wu[cols(c), :], preferred_element_type=F32)
            if c == 0:
                gate_acc[...] = gate_part
                up_acc[...] = up_part
            elif c < C - 1:
                gate_acc[...] += gate_part
                up_acc[...] += up_part
            else:
                gate_part = gate_acc[...] + gate_part
                up_part = up_acc[...] + up_part
                hid[...] = (jax.nn.silu(gate_part) * up_part).astype(BF16)

    all_rows = 2 * half
    lane = lax.broadcasted_iota(jnp.int32, (all_rows, LANES), 1)
    scale = jnp.sum(
        jnp.where(lane == me // 2, tok[:, width:width + LANES].astype(F32), 0.0),
        axis=1, keepdims=True,
    )

    sc = [remote(core_out.at[:, cols(c)], core_in.at[:, cols(c)], rc_s.at[c], rc_r.at[c], core_peer)
          for c in range(C)]
    so = [remote(y_out.at[0:rows, span], y_in.at[0:rows, span], ro_s.at[g], ro_r.at[g], y_peer)
          for g, span in enumerate([
              pl.ds(0, split * chunk), pl.ds(split * chunk, (C - split) * chunk)
          ])]
    sy = [remote(y_out.at[rows:quarter, cols(c)], y_in.at[rows:quarter, cols(c)],
                 ry_s.at[c], ry_r.at[c], y_peer) for c in range(C)]
    sz = [[remote(z_out.at[d * rows:(d + 1) * rows, cols(c)],
                  z_in.at[(Z - d) * rows:(Z - d + 1) * rows, cols(c)],
                  rz_s.at[c, d], rz_r.at[c, Z - d], z_peer[d]) for d in range(1, Z)]
          for c in range(C)]

    for step in range(C + 2):
        if step < C:
            c = step
            load_down[c].wait()
            if c == 0:
                part = jnp.dot(hid[half:, :], wd[:, cols(c)], preferred_element_type=F32)
                core_out[:, cols(c)] = (scale[half:] * part).astype(BF16)
                sc[c].start()
                part = jnp.dot(hid[0:half, :], wd[:, cols(c)], preferred_element_type=F32)
                own[:, cols(c)] = scale[:half] * part
            else:
                part = scale * jnp.dot(hid[...], wd[:, cols(c)], preferred_element_type=F32)
                core_out[:, cols(c)] = part[half:].astype(BF16)
                sc[c].start()
                own[:, cols(c)] = part[:half]
        if 0 <= step - 1 < C:
            c = step - 1
            sc[c].wait_recv()
            total = own[:, cols(c)] + core_in[:, cols(c)].astype(F32)
            y_out[:, cols(c)] = total[quarter:].astype(BF16)
            sy[c].start()
            own[0:quarter, cols(c)] = total[:quarter]
            if c == C - 1:
                for copy in so:
                    copy.start()
        if 0 <= step - 2 < C:
            c = step - 2
            sy[c].wait_recv()
            total = own[rows:quarter, cols(c)] + y_in[rows:, cols(c)].astype(F32)
            z_out[rows:, cols(c)] = total.astype(BF16)
            for copy in sz[c]:
                copy.start()
    for c in range(C):
        if c in (0, split):
            so[c // split].wait_recv()
        for copy in sz[c]:
            copy.wait_recv()
        total = own[0:rows, cols(c)] + y_in[0:rows, cols(c)].astype(F32)
        for d in range(1, Z):
            total = total + z_in[d * rows:(d + 1) * rows, cols(c)].astype(F32)
        out_ref[:, cols(c)] = total.astype(BF16)

    for c in range(C):
        each_z(c, wait_send)
        each_relay(c, wait_send)
        for copy in [gy[c], gc[c], sc[c], sy[c]] + sz[c]:
            copy.wait_send()
    for copy in go + so:
        copy.wait_send()


def per_device(tokens, expert_ids, gates, expert_place, gate_proj, up_proj, down_proj):
    nodes = lax.axis_size("node")
    Z = nodes // 4
    C = 7
    rows, width = tokens.shape
    units = gate_proj.shape[1]
    all_rows = nodes * rows
    dma = pltpu.SemaphoreType.DMA
    vmem = pl.BlockSpec(memory_space=pltpu.VMEM)
    hbm = pl.BlockSpec(memory_space=pl.ANY)
    return pl.pallas_call(
        functools.partial(kernel, Z, C),
        out_shape=jax.ShapeDtypeStruct((rows, width), BF16),
        in_specs=[pl.BlockSpec(memory_space=pltpu.SMEM), vmem, vmem, hbm, hbm, hbm, hbm],
        out_specs=vmem,
        scratch_shapes=[
            pltpu.VMEM((all_rows, width + LANES), BF16),
            pltpu.VMEM((width, units), BF16),
            pltpu.VMEM((width, units), BF16),
            pltpu.VMEM((units, width), BF16),
            pltpu.VMEM((all_rows, units), F32),
            pltpu.VMEM((all_rows, units), F32),
            pltpu.VMEM((all_rows, units), BF16),
            pltpu.VMEM((all_rows // 2, width), F32),
            pltpu.VMEM((all_rows // 2, width), BF16),
            pltpu.VMEM((all_rows // 2, width), BF16),
            pltpu.VMEM((all_rows // 4, width), BF16),
            pltpu.VMEM((all_rows // 4, width), BF16),
            pltpu.VMEM((all_rows // 4, width), BF16),
            pltpu.VMEM((all_rows // 4, width), BF16),
            dma, dma((C,)), dma((C,)), dma((C,)),
            dma((C, Z)), dma((C, Z)), dma((C,)), dma((2,)), dma((2,)),
            dma((C,)), dma((C,)), dma((C,)), dma((C,)),
            dma((C,)), dma((C,)), dma((2,)), dma((2,)), dma((C,)), dma((C,)), dma((C, Z)), dma((C, Z)),
        ],
        compiler_params=pltpu.CompilerParams(
            collective_id=0, has_side_effects=True, vmem_limit_bytes=60 * 2 ** 20
        ),
        cost_estimate=pl.CostEstimate(
            flops=6 * all_rows * width * units,
            bytes_accessed=6 * width * units,
            transcendentals=all_rows * units,
        ),
    )(expert_place, expert_ids.T, gates.T, tokens, gate_proj, up_proj, down_proj)


def solution(mesh):
    placed = (
        P(("group", "node"), None),
        P(("group", "node"), None),
        P(("group", "node"), None),
        P(),
        P(None, "node"),
        P(None, "node"),
        P("node", None),
    )
    return jax.shard_map(
        per_device,
        mesh=mesh,
        in_specs=placed,
        out_specs=P(("group", "node"), None),
        check_vma=False,
    )
```
